512 devices in a mesh: queue: 32 (over z, y_hi), tensor: 16 (over x, y_lo, core).
Axes of the slice: x: 4, y: 4 (y_hi: 2, y_lo: 2; y = y_hi * 2 + y_lo), z: 16, core: 2. Of those that a mesh axis runs over, the one named last changes fastest.
Arguments:
- frames_in: bfloat16 [32, 384, 3072], P('queue', None, 'tensor'), may hold values from -6 to 6
- fresh: bfloat16 [384, 3072], P(None, 'tensor'), may hold values from -6 to 6
- levels: int32 [32], P('queue'), may hold values from 0 to 127, as said below
- reach: int32 [32], P('queue'), may hold values from 0 to 3
- level_mod: bfloat16 [128, 3, 3072], P(None, None, 'tensor'), may hold values from -3 to 3
- w_qkv: bfloat16 [3072, 3, 2048], P(None, None, 'tensor')
- q_gain: float32 [2048], P('tensor'), as said below
- k_gain: float32 [2048], P('tensor'), as said below
- w_out: bfloat16 [2048, 3072], P('tensor'), may hold values from -0.75 to 0.75
Outputs:
- frames_out: bfloat16 [32, 384, 3072], P('queue', None, 'tensor')
The draws below stay inside these ranges and needn't reach their ends.
Inputs may be any that keep to these rules, and one draw needn't show every extreme that they name: levels[f] lies in [f * 4, (f + 1) * 4), so levels rise with the slot. `q_gain`: positive. `k_gain`: positive.
All inputs are finite; a program needn't handle non-finite values.
Results may differ from the reference program's by a relative error of at most 0.008.
The reference program's roundings to bfloat16 on the way count: a program that leaves them out, or rounds other values in their place, can miss the bound.
Values may be sent and summed in bfloat16 or wider, within the bound.
A program may use at most 64 MiB of HBM per device.

```python
import jax
import jax.numpy as jnp
from jax import lax

D = 3072
HEADS = 16
HD = 128
TOK = 384
REACH = 3
LEV_SLOT = 4
FRAMES = 32
LEVELS = 128


def ramped(key, shape, rise):
    column = jnp.arange(D, dtype=jnp.float32) / D
    factor = jnp.exp(rise * column)
    return jnp.clip(jax.random.normal(key, shape, jnp.float32) * factor, -6.0, 6.0)


def draw_frames_in(key, part):
    key = jax.random.fold_in(key, 21)
    return ramped(key, (FRAMES, TOK, D), 0.55).astype(jnp.bfloat16)


def draw_fresh(key, part):
    key = jax.random.fold_in(key, 22)
    return ramped(key, (TOK, D), 0.55).astype(jnp.bfloat16)


def draw_w_qkv(key, part):
    key = jax.random.fold_in(key, 23)
    main_key = jax.random.fold_in(key, 0)
    factor = D ** (-0.5)
    weights = jnp.clip(jax.random.normal(main_key, (D, 3, HEADS * HD), jnp.float32), -6.0, 6.0) * factor
    return weights.astype(jnp.bfloat16)


def draw_levels(key, part):
    key = jax.random.fold_in(key, 11)
    offset = jax.random.randint(key, (FRAMES,), 0, LEV_SLOT)
    slots = jnp.arange(FRAMES, dtype=jnp.int32)
    offset = jnp.where(slots == 0, 0, jnp.where(slots == FRAMES - 1, LEV_SLOT - 1, offset))
    return (slots * LEV_SLOT + offset).astype(jnp.int32)


def draw_reach(key, part):
    key = jax.random.fold_in(key, 12)
    value_key, order_key = jax.random.split(key)
    values = jax.random.randint(value_key, (FRAMES,), 0, REACH + 1)
    order = jax.random.permutation(order_key, FRAMES)
    values = values.at[order[0]].set(REACH)
    values = values.at[order[1]].set(0)
    return values.astype(jnp.int32)


def gain_values(key, lowest, highest):
    return jnp.exp(jax.random.uniform(key, (HEADS * HD,), jnp.float32, jnp.log(lowest), jnp.log(highest)))


def draw_q_gain(key, part):
    key = jax.random.fold_in(key, 13)
    return gain_values(key, 1.0, 3.0)


def draw_k_gain(key, part):
    key = jax.random.fold_in(key, 14)
    return gain_values(key, 1.0, 3.0)


def with_spikes(values, own_key, source, target, blocks, factor):
    owner, partner = [(jnp.arange(values.shape[position]) // (values.shape[position] // blocks)).reshape([-1 if axis == position else 1 for axis in range(values.ndim)]) for position in (source, target)]
    chosen = jax.random.permutation(own_key, blocks)[partner]
    strong = (owner == chosen) | (owner == (partner + blocks // 2) % blocks)
    return jnp.where(strong, factor * values, values)


def steps_of(own_key, shape, shards, low, largest):
    def one(dim, shards_of):
        steps = jax.random.uniform(jax.random.fold_in(jax.random.fold_in(own_key, 6), dim), (shards_of,), jnp.float32, low / len(shards), largest / len(shards))
        return jnp.repeat(jnp.exp(steps), shape[dim] // shards_of).reshape((-1,) + (1,) * (len(shape) - dim - 1))

    level = one(*shards[0])
    for cut in shards[1:]:
        level = level * one(*cut)
    return level


def bell_draw(stream_key, dims, scale, most, cuts=(), kind=jnp.bfloat16):
    array = scale * jax.random.normal(stream_key, dims, jnp.float32)
    if cuts:
        array = array * steps_of(stream_key, dims, cuts, -0.22, 0.18)
    return jnp.clip(array, -most, most).astype(kind)


def gaussian_with(rng, dims, scale, limit, shards, heavy, held_as=jnp.bfloat16):
    entries = scale * jax.random.normal(rng, dims, jnp.float32)
    if shards:
        entries = entries * steps_of(rng, dims, shards, -0.22, 0.18)
    return jnp.clip(with_spikes(entries, jax.random.fold_in(rng, 3), *heavy), -limit, limit).astype(held_as)


def setup_inputs(seed: int = 0) -> dict:
    arg_keys = jax.random.split(jax.random.key(seed), 10)
    frames_in = draw_frames_in(jax.random.fold_in(arg_keys[9], 71), 0)
    fresh = draw_fresh(jax.random.fold_in(arg_keys[9], 71), 0)
    levels = draw_levels(jax.random.fold_in(arg_keys[9], 71), 0)
    reach = draw_reach(jax.random.fold_in(arg_keys[9], 71), 0)
    level_mod = bell_draw(arg_keys[4], (LEVELS, 3, D), 0.5, 3.0, ((2, 16),))
    w_qkv = draw_w_qkv(jax.random.fold_in(arg_keys[9], 71), 0)
    q_gain = draw_q_gain(jax.random.fold_in(arg_keys[9], 71), 0)
    k_gain = draw_k_gain(jax.random.fold_in(arg_keys[9], 71), 0)
    w_out = gaussian_with(arg_keys[8], (HEADS * HD, D), HD ** -0.5, 0.75, ((0, 16),), (0, 1, 16, 2.0))
    return {"frames_in": frames_in, "fresh": fresh, "levels": levels, "reach": reach, "level_mod": level_mod, "w_qkv": w_qkv, "q_gain": q_gain, "k_gain": k_gain, "w_out": w_out}


EPS = 1e-06

def rms_gain(values, gain):
    power = lax.optimization_barrier(jnp.mean(values * values, axis=-1, keepdims=True))
    return values * lax.rsqrt(power + EPS) * gain

def reference(frames_in, fresh, levels, reach, level_mod, w_qkv, q_gain, k_gain, w_out):
    shifted = jnp.concatenate([fresh[None], frames_in[:-1]], axis=0)
    onehot = (levels[:, None] == jnp.arange(LEVELS, dtype=jnp.int32)[None, :]).astype(jnp.float32)
    modulation = jnp.einsum('fl,lcd->fcd', onehot, level_mod.astype(jnp.float32), precision=lax.Precision.HIGHEST)
    latent = shifted.astype(jnp.float32)
    center = lax.optimization_barrier(jnp.mean(latent, axis=-1, keepdims=True))
    spread = lax.optimization_barrier(jnp.mean((latent - center) ** 2, axis=-1, keepdims=True))
    normed = (latent - center) * lax.rsqrt(spread + EPS)
    hidden = (normed * (1.0 + modulation[:, 1][:, None, :]) + modulation[:, 0][:, None, :]).astype(jnp.bfloat16)
    packed = jnp.dot(hidden.reshape(FRAMES * TOK, D), w_qkv.reshape(D, 3 * HEADS * HD), preferred_element_type=jnp.float32)
    packed = packed.reshape(FRAMES, TOK, 3, HEADS, HD)
    query = rms_gain(packed[:, :, 0], q_gain.reshape(HEADS, HD)).astype(jnp.bfloat16)
    keyed = rms_gain(packed[:, :, 1], k_gain.reshape(HEADS, HD)).astype(jnp.bfloat16)
    valued = packed[:, :, 2].astype(jnp.bfloat16)
    pad_width = ((REACH, REACH), (0, 0), (0, 0), (0, 0))
    key_pad = jnp.pad(keyed, pad_width)
    value_pad = jnp.pad(valued, pad_width)
    offsets = jnp.arange(2 * REACH + 1, dtype=jnp.int32) - REACH

    def one_frame(frame):
        frame_keys = lax.dynamic_slice_in_dim(key_pad, frame, 2 * REACH + 1, 0)
        frame_values = lax.dynamic_slice_in_dim(value_pad, frame, 2 * REACH + 1, 0)
        target = frame + offsets
        usable = (jnp.abs(offsets) <= reach[frame]) & (target >= 0) & (target < FRAMES)
        frame_rows = lax.dynamic_index_in_dim(query, frame, 0, keepdims=False)

        def one_head(head):
            head_rows = lax.dynamic_index_in_dim(frame_rows, head, 1, keepdims=False).astype(jnp.float32)
            head_keys = lax.dynamic_index_in_dim(frame_keys, head, 2, keepdims=False).astype(jnp.float32)
            head_values = lax.dynamic_index_in_dim(frame_values, head, 2, keepdims=False).astype(jnp.float32)
            scores = jnp.einsum('td,psd->tps', head_rows, head_keys) * HD ** (-0.5)
            scores = jnp.where(usable[None, :, None], scores, -jnp.inf)
            highest = lax.optimization_barrier(jnp.max(scores, axis=(1, 2), keepdims=True))
            expd = jnp.exp(scores - highest)
            weights = (expd / lax.optimization_barrier(jnp.sum(expd, axis=(1, 2), keepdims=True))).astype(jnp.bfloat16)
            mixed = jnp.einsum('tps,psd->td', weights.astype(jnp.float32), head_values)
            return mixed.astype(jnp.bfloat16)
        per_head = lax.map(one_head, jnp.arange(HEADS, dtype=jnp.int32))
        return jnp.transpose(per_head, (1, 0, 2)).reshape(TOK, HEADS * HD)
    attn = lax.map(one_frame, jnp.arange(FRAMES, dtype=jnp.int32))
    proj = jnp.dot(attn.reshape(FRAMES * TOK, HEADS * HD), w_out, preferred_element_type=jnp.float32).reshape(FRAMES, TOK, D)
    result = latent + modulation[:, 2][:, None, :] * proj
    return result.astype(jnp.bfloat16)
```

```python
import jax
import jax.numpy as jnp
from jax import lax
from jax.experimental import pallas as pl
from jax.experimental.pallas import tpu as pltpu
from jax.sharding import PartitionSpec as P

MESH = pl.DeviceIdType.MESH
HD = 128
EPS = 1e-06
LANE = 128
F32 = jnp.float32
BF16 = jnp.bfloat16


def kernel(
    queues, levels_ref, reach_ref, frames_ref, fresh_ref, mod_ref, w_ref, qg_ref, kg_ref, wo_ref,
    out_ref,
    xs, xr, st, stb, lm, modc, wq, wt, hb, qt, kv, m_s, l_s, o_s, ab, wo_in, wo_send, wo_recv, gains,
    local_sem, ss, r_shift, r_stat, r_h, r_kv, r_ab, r_wo,
):
    blocks = xs.shape[0]
    part = xs.shape[1]
    width = 16 * part
    q = lax.axis_index("queue")
    t = lax.axis_index("tensor")
    z, e = q // 2, q % 2
    x, y, c = t // 4, (t // 2) % 2, t % 2
    zs = queues // 2

    def tid(dx, fy, fc):
        xx = (x + dx) % 4
        yy = (y + fy) % 2
        cc = (c + fc) % 2
        return xx * 4 + yy * 2 + cc

    def queue_id(dz, flip):
        return ((z + dz + zs) % zs) * 2 + (e + flip) % 2

    sends = []

    def send(src, dst, recv_sem, device):
        copy = pltpu.make_async_remote_copy(
            src_ref=src, dst_ref=dst, send_sem=ss.at[len(sends)], recv_sem=recv_sem,
            device_id=device, device_id_type=MESH,
        )
        copy.start()
        sends.append(copy)

    def arrived(dst, recv_sem):
        pltpu.make_async_remote_copy(
            src_ref=dst, dst_ref=dst, send_sem=ss.at[0], recv_sem=recv_sem,
            device_id=(q, tid(0, 0, 1)), device_id_type=MESH,
        ).wait_recv()

    last = q == queues - 1
    loads = []

    def load(src, dst):
        copy = pltpu.make_async_copy(src, dst, local_sem.at[len(loads)])
        loads.append(copy)
        return copy

    for j in range(blocks):
        lanes = pl.ds(j * LANE, LANE)
        from_queue = load(frames_ref.at[:, lanes], xs.at[j])
        from_noise = pltpu.make_async_copy(fresh_ref.at[:, lanes], xs.at[j], local_sem.at[j])

        @pl.when(last)
        def _():
            from_noise.start()

        @pl.when(jnp.logical_not(last))
        def _():
            from_queue.start()

    load_mod = load(mod_ref, lm)
    load_w = load(w_ref, wq)
    load_wo = load(wo_ref, wo_in)
    load_qg = load(qg_ref, gains.at[pl.ds(0, 1)])
    load_kg = load(kg_ref, gains.at[pl.ds(8, 1)])
    for copy in (load_mod, load_w, load_wo, load_qg, load_kg):
        copy.start()

    after = (q + 1) % queues
    before = (q + queues - 1) % queues
    barrier = pltpu.get_barrier_semaphore()
    for k in range(1, 16):
        pl.semaphore_signal(barrier, inc=1, device_id=(q, (t + k) % 16), device_id_type=MESH)
    for k in range(16):
        pl.semaphore_signal(barrier, inc=1, device_id=(after, (t + k) % 16), device_id_type=MESH)
        pl.semaphore_signal(barrier, inc=1, device_id=(before, (t + k) % 16), device_id_type=MESH)
    for dz in (1, -1):
        pl.semaphore_signal(barrier, inc=1, device_id=(queue_id(dz, 0), t), device_id_type=MESH)

    for j in range(blocks):
        loads[j].wait()
        values = xs[j].astype(F32)
        total = jnp.sum(values, axis=0, keepdims=True)
        rest = values - total * (1.0 / part)
        st[j : j + 1, :] = total
        st[blocks + j : blocks + j + 1, :] = jnp.sum(rest * rest, axis=0, keepdims=True)
    pl.semaphore_wait(barrier, 15 + 32 + 2)

    send(xs.at[0], xr.at[0], r_shift.at[0], (after, t))
    for k in range(16):
        send(st, stb.at[t], r_stat.at[t], (after, (t + k) % 16))
    for j in range(1, blocks):
        send(xs.at[j], xr.at[j], r_shift.at[j], (after, t))

    load_mod.wait()
    chosen = lax.broadcasted_iota(jnp.int32, (part, LANE), 1) == levels_ref[0]
    for k in range(3):
        modc[k] = jnp.sum(jnp.where(chosen, lm[k].astype(F32), 0.0), axis=1, keepdims=True)
    load_qg.wait()
    load_kg.wait()
    eye = lax.broadcasted_iota(jnp.int32, (HD, HD), 0) == lax.broadcasted_iota(jnp.int32, (HD, HD), 1)
    q_gain = jnp.sum(jnp.where(eye, gains[0:1, :], 0.0), axis=1, keepdims=True)
    k_gain = jnp.sum(jnp.where(eye, gains[8:9, :], 0.0), axis=1, keepdims=True)

    load_w.wait()

    def turn(chip, _):
        for k in range(3):
            for piece in range(3):
                rows = pl.ds(pl.multiple_of(chip * 384 + piece * 128, 128), 128)
                wt[chip, k * 128 : (k + 1) * 128, piece * 128 : (piece + 1) * 128] = wq[k, rows, :].T
        return 0

    lax.fori_loop(0, 8, turn, 0)

    def slot_wait(j, slot):
        arrived(hb.at[j, slot], r_h.at[j, slot])

    def slot_send(j, slot, device_t):
        send(hb.at[j, slot], hb.at[j, slot], r_h.at[j, slot], (q, device_t))

    for k in range(16):
        slot = (t + k) % 16
        arrived(stb.at[slot], r_stat.at[slot])
    center = jnp.sum(stb[:, 0:blocks, :], axis=0) * (1.0 / width)
    offs = stb[:, 0:blocks, :] * (1.0 / part) - center[None]
    spread = jnp.sum(stb[:, blocks : 2 * blocks, :] + part * offs * offs, axis=0) * (1.0 / width)
    factor = lax.rsqrt(spread + EPS)

    def normalise(j):
        arrived(xr.at[j], r_shift.at[j])
        normed = (xr[j].astype(F32) - center[j : j + 1, :]) * factor[j : j + 1, :]
        hb[j, t] = (normed * (1.0 + modc[1]) + modc[0]).astype(BF16)
        for target in (tid(0, 1, 0), tid(2, 0, 0), tid(1, 0, 0), tid(3, 0, 0), tid(0, 0, 1)):
            slot_send(j, t, target)

    other = tid(0, 0, 1)

    def relay_y(j):
        slot = tid(0, 1, 0)
        slot_wait(j, slot)
        for target in (tid(1, 0, 0), tid(3, 0, 0), other):
            slot_send(j, slot, target)

    def relay_far(j):
        slot = tid(2, 0, 0)
        slot_wait(j, slot)
        slot_send(j, slot, tid(0, 1, 0))
        slot_send(j, slot, other)

    def relay_chip(j, dx, fy):
        slot = tid(dx, fy, 0)
        slot_wait(j, slot)
        slot_send(j, slot, other)

    def early(j):
        relay_y(j)
        relay_chip(j, 1, 0)
        relay_chip(j, 3, 0)
        relay_far(j)

    def late(j):
        relay_chip(j, 1, 1)
        relay_chip(j, 3, 1)
        relay_chip(j, 2, 1)

    sigma = 2 * e - 1
    own, s_near, s_away, o_0, o_near, o_away, o_far = range(7)

    def kv_send(j, slot, there, device):
        send(kv.at[slot, j], kv.at[there, j], r_kv.at[there, j], device)

    def kv_wait(j, slot):
        arrived(kv.at[slot, j], r_kv.at[slot, j])

    def project(j):
        for dx in range(4):
            for fy in range(2):
                slot = tid(dx, fy, 1)
                slot_wait(j, slot)

        def one(chip, total):
            h = hb[j, pl.ds(2 * chip, 2)].reshape(2 * part, LANE)
            return total + jnp.dot(wt[chip], h, preferred_element_type=F32)

        packed = lax.fori_loop(0, 8, one, jnp.zeros((3 * HD, LANE), F32))
        query, keyed, valued = packed[:HD], packed[HD : 2 * HD], packed[2 * HD :]

        def rms(values, gain):
            power = jnp.mean(values * values, axis=0, keepdims=True)
            return (values * lax.rsqrt(power + EPS) * gain).astype(BF16)

        kv[own, j, 0] = rms(keyed, k_gain).T
        kv[own, j, 1] = valued.astype(BF16)
        kv_send(j, own, s_near, (queue_id(sigma, 0), t))
        kv_send(j, own, o_0, (queue_id(0, 1), t))
        kv_send(j, own, s_away, (queue_id(-sigma, 0), t))
        qt[:, j * LANE : (j + 1) * LANE] = rms(query, q_gain)

    def kv_relay_1(j):
        kv_wait(j, s_near)
        kv_send(j, s_near, o_near, (queue_id(0, 1), t))
        kv_wait(j, o_0)
        kv_send(j, o_0, o_away, (queue_id(sigma, 0), t))

    def kv_relay_2(j):
        kv_wait(j, o_near)
        kv_send(j, o_near, o_far, (queue_id(-sigma, 0), t))

    normalise(0)
    normalise(1)
    early(0)
    normalise(2)
    early(1)
    late(0)
    project(0)
    early(2)
    late(1)
    project(1)
    kv_relay_1(0)
    late(2)
    project(2)

    load_wo.wait()

    def turn_out(k, _):
        lanes = pl.ds(pl.multiple_of(k * 384, 128), 384)
        wo_send[pl.ds(2 * k, 2)] = wo_in[:, lanes].T.reshape(2, part, LANE)
        return 0

    lax.fori_loop(0, 8, turn_out, 0)
    for k in range(1, 16):
        target = (t + k) % 16
        send(wo_send.at[target], wo_recv.at[t], r_wo.at[t], (q, target))

    f = q
    scale = HD ** (-0.5)
    m_s[...] = jnp.full(m_s.shape, -jnp.inf, F32)
    l_s[...] = jnp.zeros(l_s.shape, F32)
    o_s[...] = jnp.zeros(o_s.shape, F32)

    def attend(slot, offset):
        keys = kv[slot, :, 0].reshape(blocks * LANE, HD)
        scores = jnp.dot(keys, qt[...], preferred_element_type=F32)
        frame = f + offset
        usable = (jnp.abs(offset) <= reach_ref[0]) & (frame >= 0) & (frame < queues)
        scores = scores * scale + jnp.where(usable, 0.0, -jnp.inf).astype(F32)
        m_old = m_s[0:1, :]
        m_new = jnp.maximum(m_old, jnp.max(scores, axis=0, keepdims=True))
        weights = jnp.exp(scores - m_new)
        fade = jnp.exp(m_old - m_new)
        l_s[0:1, :] = l_s[0:1, :] * fade + jnp.sum(weights, axis=0, keepdims=True)
        m_s[0:1, :] = m_new
        half = weights.astype(BF16)
        values = jnp.concatenate([kv[slot, j, 1] for j in range(blocks)], axis=1)
        o_s[...] = o_s[...] * fade + jnp.dot(values, half, preferred_element_type=F32)

    kv_relay_1(1)
    kv_relay_2(0)
    attend(own, 0)
    kv_relay_1(2)
    kv_relay_2(1)
    attend(s_near, -2 * sigma)
    attend(o_0, -sigma)
    kv_relay_2(2)
    attend(o_near, sigma)
    for j in range(blocks):
        kv_wait(j, s_away)
    attend(s_away, 2 * sigma)
    for j in range(blocks):
        kv_wait(j, o_away)
    attend(o_away, -3 * sigma)
    for j in range(blocks):
        kv_wait(j, o_far)
    attend(o_far, 3 * sigma)

    ab[t] = (o_s[...] / l_s[0:1, :]).astype(BF16)

    def ab_send(slot, target):
        send(ab.at[slot], ab.at[slot], r_ab.at[slot], (q, target))

    def ab_wait(slot):
        arrived(ab.at[slot], r_ab.at[slot])

    for target in (tid(0, 1, 0), tid(2, 0, 0), tid(1, 0, 0), tid(3, 0, 0), other):
        ab_send(t, target)
    for k in range(1, 16):
        source = (t + k) % 16
        arrived(wo_recv.at[source], r_wo.at[source])
    wo_recv[t] = wo_send[t]
    slot = tid(0, 1, 0)
    ab_wait(slot)
    for target in (tid(1, 0, 0), tid(3, 0, 0), other):
        ab_send(slot, target)
    for dx in (1, 3):
        slot = tid(dx, 0, 0)
        ab_wait(slot)
        ab_send(slot, other)
    slot = tid(2, 0, 0)
    ab_wait(slot)
    ab_send(slot, tid(0, 1, 0))
    ab_send(slot, other)
    for dx in (1, 3, 2):
        slot = tid(dx, 1, 0)
        ab_wait(slot)
        ab_send(slot, other)
    for dx in range(4):
        for fy in range(2):
            ab_wait(tid(dx, fy, 1))

    def mix(k, total):
        weights = jnp.concatenate([wo_recv[2 * k], wo_recv[2 * k + 1]], axis=1)
        heads = ab[pl.ds(2 * k, 2)].reshape(2 * HD, blocks * LANE)
        return total + jnp.dot(weights, heads, preferred_element_type=F32)

    proj = lax.fori_loop(0, 8, mix, jnp.zeros((part, blocks * LANE), F32))
    for j in range(blocks):
        lanes = slice(j * LANE, (j + 1) * LANE)
        out_ref[:, lanes] = (xr[j].astype(F32) + modc[2] * proj[:, lanes]).astype(BF16)
    for copy in sends:
        copy.wait_send()


def local(frames_in, fresh, levels, reach, level_mod, w_qkv, q_gain, k_gain, w_out):
    queues = lax.axis_size("queue")
    tokens, part = fresh.shape
    model = w_qkv.shape[0]
    blocks = tokens // LANE
    vmem = pltpu.VMEM
    dma = pltpu.SemaphoreType.DMA
    any_spec = pl.BlockSpec(memory_space=pl.ANY)
    smem_spec = pl.BlockSpec(memory_space=pltpu.SMEM)
    out = pl.pallas_call(
        lambda *refs: kernel(queues, *refs),
        out_shape=jax.ShapeDtypeStruct((part, tokens), BF16),
        in_specs=[smem_spec, smem_spec] + [any_spec] * 7,
        out_specs=pl.BlockSpec(memory_space=pltpu.VMEM),
        scratch_shapes=[
            vmem((blocks, part, LANE), BF16),
            vmem((blocks, part, LANE), BF16),
            vmem((8, LANE), F32),
            vmem((16, 8, LANE), F32),
            vmem((3, part, LANE), BF16),
            vmem((3, part, 1), F32),
            vmem((3, model, LANE), BF16),
            vmem((8, 3 * HD, 2 * part), BF16),
            vmem((blocks, 16, part, LANE), BF16),
            vmem((HD, tokens), BF16),
            vmem((7, blocks, 2, HD, HD), BF16),
            vmem((8, tokens), F32),
            vmem((8, tokens), F32),
            vmem((HD, tokens), F32),
            vmem((16, HD, tokens), BF16),
            vmem((HD, model), BF16),
            vmem((16, part, HD), BF16),
            vmem((16, part, HD), BF16),
            vmem((16, LANE), F32),
            dma((16,)),
            dma((128,)),
            dma((blocks,)),
            dma((16,)),
            dma((blocks, 16)),
            dma((7, blocks)),
            dma((16,)),
            dma((16,)),
        ],
        compiler_params=pltpu.CompilerParams(
            collective_id=0, has_side_effects=True, vmem_limit_bytes=56 * 1024 * 1024
        ),
        name="block",
    )(
        levels, reach, frames_in[0].T, fresh.T, jnp.transpose(level_mod, (1, 2, 0)),
        jnp.transpose(w_qkv, (1, 0, 2)), q_gain.reshape(1, HD), k_gain.reshape(1, HD), w_out,
    )
    return out.T[None]


def solution(mesh):
    return jax.shard_map(
        local,
        mesh=mesh,
        in_specs=(
            P("queue", None, "tensor"),
            P(None, "tensor"),
            P("queue"),
            P("queue"),
            P(None, None, "tensor"),
            P(None, None, "tensor"),
            P("tensor"),
            P("tensor"),
            P("tensor", None),
        ),
        out_specs=P("queue", None, "tensor"),
        check_vma=False,
    )
```

```python
import jax
import jax.numpy as jnp
from jax import lax
from jax.experimental import pallas as pl
from jax.experimental.pallas import tpu as pltpu
from jax.sharding import PartitionSpec as P

MESH = pl.DeviceIdType.MESH
HD = 128
EPS = 1e-06
LANE = 128
F32 = jnp.float32
BF16 = jnp.bfloat16


def kernel(
    queues, levels_ref, reach_ref, frames_ref, fresh_ref, mod_ref, w_ref, qg_ref, kg_ref, wo_ref,
    out_ref,
    xs, xr, st, stb, lm, modc, wq, wt, hb, qt, kv, m_s, l_s, o_s, ab, wo_in, wo_send, wo_recv, gains,
    level_s, reach_s, local_sem, ss, r_shift, r_stat, r_h, r_kv, r_ab, r_wo,
):
    blocks = xs.shape[0]
    part = xs.shape[1]
    width = 16 * part
    q = lax.axis_index("queue")
    t = lax.axis_index("tensor")
    z, e = q // 2, q % 2
    x, y, c = t // 4, (t // 2) % 2, t % 2
    zs = queues // 2

    def tid(dx, fy, fc):
        xx = (x + dx) % 4
        yy = (y + fy) % 2
        cc = (c + fc) % 2
        return xx * 4 + yy * 2 + cc

    def queue_id(dz, flip):
        return ((z + dz + zs) % zs) * 2 + (e + flip) % 2

    sends = []

    def send(src, dst, recv_sem, device):
        copy = pltpu.make_async_remote_copy(
            src_ref=src, dst_ref=dst, send_sem=ss.at[len(sends)], recv_sem=recv_sem,
            device_id=device, device_id_type=MESH,
        )
        copy.start()
        sends.append(copy)

    def arrived(dst, recv_sem):
        pltpu.make_async_remote_copy(
            src_ref=dst, dst_ref=dst, send_sem=ss.at[0], recv_sem=recv_sem,
            device_id=(q, tid(0, 0, 1)), device_id_type=MESH,
        ).wait_recv()

    last = q == queues - 1
    loads = []

    def load(src, dst):
        copy = pltpu.make_async_copy(src, dst, local_sem.at[len(loads)])
        loads.append(copy)
        return copy

    for j in range(blocks):
        lanes = pl.ds(j * LANE, LANE)
        from_queue = load(frames_ref.at[:, lanes], xs.at[j])
        from_noise = pltpu.make_async_copy(fresh_ref.at[:, lanes], xs.at[j], local_sem.at[j])

        @pl.when(last)
        def _():
            from_noise.start()

        @pl.when(jnp.logical_not(last))
        def _():
            from_queue.start()

    load_wo = load(wo_ref, wo_in)
    load_level = load(levels_ref, level_s)
    load_reach = load(reach_ref, reach_s)
    load_mod = load(mod_ref, lm)
    load_w = load(w_ref, wq)
    load_qg = load(qg_ref, gains.at[pl.ds(0, 1)])
    load_kg = load(kg_ref, gains.at[pl.ds(8, 1)])
    for copy in loads[blocks:]:
        copy.start()

    after = (q + 1) % queues
    before = (q + queues - 1) % queues
    barrier = pltpu.get_barrier_semaphore()
    for k in range(1, 16):
        pl.semaphore_signal(barrier, inc=1, device_id=(q, (t + k) % 16), device_id_type=MESH)
    for k in range(16):
        pl.semaphore_signal(barrier, inc=1, device_id=(after, (t + k) % 16), device_id_type=MESH)
        pl.semaphore_signal(barrier, inc=1, device_id=(before, (t + k) % 16), device_id_type=MESH)
    for dz in (1, -1):
        pl.semaphore_signal(barrier, inc=1, device_id=(queue_id(dz, 0), t), device_id_type=MESH)
    sigma = 2 * e - 1
    pl.semaphore_signal(barrier, inc=1, device_id=(queue_id(2 * sigma, 1), t), device_id_type=MESH)

    for j in range(blocks):
        loads[j].wait()
        values = xs[j].astype(F32)
        total = jnp.sum(values, axis=0, keepdims=True)
        rest = values - total * (1.0 / part)
        st[j : j + 1, :] = total
        st[blocks + j : blocks + j + 1, :] = jnp.sum(rest * rest, axis=0, keepdims=True)
    pl.semaphore_wait(barrier, 15 + 32 + 3)

    send(xs.at[0], xr.at[0], r_shift.at[0], (after, t))
    for k in range(16):
        send(st, stb.at[t], r_stat.at[t], (after, (t + k) % 16))
    for j in range(1, blocks):
        send(xs.at[j], xr.at[j], r_shift.at[j], (after, t))

    load_wo.wait()

    def turn_out(k, _):
        lanes = pl.ds(pl.multiple_of(k * 384, 128), 384)
        wo_send[pl.ds(2 * k, 2)] = wo_in[:, lanes].T.reshape(2, part, LANE)
        return 0

    lax.fori_loop(0, 8, turn_out, 0)

    def send_out(across, steps):
        for dx in steps:
            for fc in range(2):
                if across:
                    target = tid(dx, 1, fc)
                    send(wo_send.at[target], wo_recv.at[t], r_wo.at[t], (queue_id(0, fc), target))
                elif dx or fc:
                    target = tid(dx, 0, fc)
                    send(wo_send.at[target], wo_recv.at[t], r_wo.at[t], (q, target))

    send_out(False, (2, 1, 3, 0))

    load_level.wait()
    load_reach.wait()
    load_mod.wait()
    chosen = lax.broadcasted_iota(jnp.int32, (part, LANE), 1) == level_s[0]
    for k in range(3):
        modc[k] = jnp.sum(jnp.where(chosen, lm[k].astype(F32), 0.0), axis=1, keepdims=True)
    load_qg.wait()
    load_kg.wait()
    eye = lax.broadcasted_iota(jnp.int32, (HD, HD), 0) == lax.broadcasted_iota(jnp.int32, (HD, HD), 1)
    q_gain = jnp.sum(jnp.where(eye, gains[0:1, :], 0.0), axis=1, keepdims=True)
    k_gain = jnp.sum(jnp.where(eye, gains[8:9, :], 0.0), axis=1, keepdims=True)

    load_w.wait()

    def turn(chip, _):
        for k in range(3):
            for piece in range(3):
                rows = pl.ds(pl.multiple_of(chip * 384 + piece * 128, 128), 128)
                wt[chip, k * 128 : (k + 1) * 128, piece * 128 : (piece + 1) * 128] = wq[k, rows, :].T
        return 0

    lax.fori_loop(0, 8, turn, 0)

    def slot_wait(buf, sems, j, slot):
        arrived(buf.at[j, slot], sems.at[j, slot])

    def slot_send(buf, sems, j, slot, device_t):
        send(buf.at[j, slot], buf.at[j, slot], sems.at[j, slot], (q, device_t))

    other = tid(0, 0, 1)
    order = ((0, 0), (0, 1), (1, 0), (3, 0), (2, 0), (1, 1), (3, 1), (2, 1))

    def gather_own(buf, sems, j):
        for target in (tid(0, 1, 0), tid(2, 0, 0), tid(1, 0, 0), tid(3, 0, 0), other):
            slot_send(buf, sems, j, t, target)

    def relay_y(buf, sems, j):
        slot = tid(0, 1, 0)
        slot_wait(buf, sems, j, slot)
        for target in (tid(1, 0, 0), tid(3, 0, 0), other):
            slot_send(buf, sems, j, slot, target)

    def relay_far(buf, sems, j):
        slot = tid(2, 0, 0)
        slot_wait(buf, sems, j, slot)
        slot_send(buf, sems, j, slot, tid(0, 1, 0))
        slot_send(buf, sems, j, slot, other)

    def relay_chip(buf, sems, j, dx, fy):
        slot = tid(dx, fy, 0)
        slot_wait(buf, sems, j, slot)
        slot_send(buf, sems, j, slot, other)

    def relay_sides(buf, sems, j):
        relay_chip(buf, sems, j, 1, 0)
        relay_chip(buf, sems, j, 3, 0)

    def late(buf, sems, j):
        relay_chip(buf, sems, j, 1, 1)
        relay_chip(buf, sems, j, 3, 1)
        relay_chip(buf, sems, j, 2, 1)

    for k in range(16):
        slot = (t + k) % 16
        arrived(stb.at[slot], r_stat.at[slot])
    center = jnp.sum(stb[:, 0:blocks, :], axis=0) * (1.0 / width)
    offs = stb[:, 0:blocks, :] * (1.0 / part) - center[None]
    spread = jnp.sum(stb[:, blocks : 2 * blocks, :] + part * offs * offs, axis=0) * (1.0 / width)
    factor = lax.rsqrt(spread + EPS)

    def normalise(j):
        arrived(xr.at[j], r_shift.at[j])
        normed = (xr[j].astype(F32) - center[j : j + 1, :]) * factor[j : j + 1, :]
        hb[j, t] = (normed * (1.0 + modc[1]) + modc[0]).astype(BF16)
        gather_own(hb, r_h, j)

    own, s_near, s_away, o_0, o_near, o_away, o_far = range(7)

    def kv_send(j, slot, there, device):
        send(kv.at[slot, j], kv.at[there, j], r_kv.at[there, j], device)

    def kv_wait(j, slot):
        arrived(kv.at[slot, j], r_kv.at[slot, j])

    def project(j):
        def one(chip, total):
            h = hb[j, pl.ds(2 * chip, 2)].reshape(2 * part, LANE)
            return total + jnp.dot(wt[chip], h, preferred_element_type=F32)

        packed = jnp.zeros((3 * HD, LANE), F32)
        for dx, fy in order:
            slot_wait(hb, r_h, j, tid(dx, fy, 1))
            packed = one(tid(dx, fy, 0) // 2, packed)
        query, keyed, valued = packed[:HD], packed[HD : 2 * HD], packed[2 * HD :]

        def rms(values, gain):
            power = jnp.mean(values * values, axis=0, keepdims=True)
            return (values * lax.rsqrt(power + EPS) * gain).astype(BF16)

        kv[own, j, 0] = rms(keyed, k_gain).T
        kv[own, j, 1] = valued.astype(BF16)
        kv_send(j, own, s_near, (queue_id(sigma, 0), t))
        kv_send(j, own, o_0, (queue_id(0, 1), t))
        if j == blocks - 1:
            kv_send(j, own, o_far, (queue_id(2 * sigma, 1), t))
        kv_send(j, own, s_away, (queue_id(-sigma, 0), t))
        qt[:, j * LANE : (j + 1) * LANE] = rms(query, q_gain)

    def kv_relay_1(j):
        kv_wait(j, s_near)
        kv_send(j, s_near, o_near, (queue_id(0, 1), t))
        kv_wait(j, o_0)
        kv_send(j, o_0, o_away, (queue_id(sigma, 0), t))

    def kv_relay_2(j):
        kv_wait(j, o_near)
        kv_send(j, o_near, o_far, (queue_id(-sigma, 0), t))

    normalise(0)
    normalise(1)
    relay_y(hb, r_h, 0)
    normalise(2)
    relay_far(hb, r_h, 0)
    relay_y(hb, r_h, 1)
    relay_sides(hb, r_h, 0)
    relay_far(hb, r_h, 1)
    relay_y(hb, r_h, 2)
    relay_sides(hb, r_h, 1)
    late(hb, r_h, 0)
    relay_far(hb, r_h, 2)
    project(0)
    relay_sides(hb, r_h, 2)
    late(hb, r_h, 1)
    project(1)
    kv_relay_1(0)
    late(hb, r_h, 2)
    project(2)
    kv_relay_1(1)
    kv_relay_2(0)

    f = q
    scale = HD ** (-0.5)
    m_s[...] = jnp.full(m_s.shape, -jnp.inf, F32)
    l_s[...] = jnp.zeros(l_s.shape, F32)
    o_s[...] = jnp.zeros(o_s.shape, F32)

    def attend(slot, offset, span=(0, 3)):
        lanes = slice(span[0] * LANE, span[1] * LANE)
        keys = kv[slot, :, 0].reshape(blocks * LANE, HD)
        scores = jnp.dot(keys, qt[:, lanes], preferred_element_type=F32)
        frame = f + offset
        usable = (jnp.abs(offset) <= reach_s[0]) & (frame >= 0) & (frame < queues)
        scores = scores * scale + jnp.where(usable, 0.0, -jnp.inf).astype(F32)
        m_old = m_s[0:1, lanes]
        m_new = jnp.maximum(m_old, jnp.max(scores, axis=0, keepdims=True))
        weights = jnp.exp(scores - m_new)
        fade = jnp.exp(m_old - m_new)
        l_s[0:1, lanes] = l_s[0:1, lanes] * fade + jnp.sum(weights, axis=0, keepdims=True)
        m_s[0:1, lanes] = m_new
        half = weights.astype(BF16)
        values = jnp.concatenate([kv[slot, j, 1] for j in range(blocks)], axis=1)
        o_s[:, lanes] = o_s[:, lanes] * fade + jnp.dot(values, half, preferred_element_type=F32)

    attend(own, 0)
    kv_relay_1(2)
    kv_relay_2(1)
    send_out(True, (2, 1, 3, 0))
    attend(s_near, -2 * sigma)
    attend(o_0, -sigma)
    for slot, offset in ((s_away, 2 * sigma), (o_far, 3 * sigma)):
        for j in range(blocks):
            kv_wait(j, slot)
        attend(slot, offset)
    kv_wait(blocks - 1, o_near)
    attend(o_near, sigma)
    for j in range(blocks):
        kv_wait(j, o_away)

    def finish(j):
        attend(o_away, -3 * sigma, (j, j + 1))
        lanes = slice(j * LANE, (j + 1) * LANE)
        ab[j, t] = (o_s[:, lanes] / l_s[0:1, lanes]).astype(BF16)
        gather_own(ab, r_ab, j)

    def out_wait(dx, fy, fc):
        if dx or fy or fc:
            source = tid(dx, fy, fc)
            arrived(wo_recv.at[source], r_wo.at[source])

    def mix(j):
        total = jnp.zeros((part, LANE), F32)
        for dx, fy in order:
            slot_wait(ab, r_ab, j, tid(dx, fy, 1))
            if j == 0:
                out_wait(dx, fy, 0)
                out_wait(dx, fy, 1)
            k = tid(dx, fy, 0) // 2
            weights = jnp.concatenate([wo_recv[2 * k], wo_recv[2 * k + 1]], axis=1)
            heads = ab[j, pl.ds(2 * k, 2)].reshape(2 * HD, LANE)
            total = total + jnp.dot(weights, heads, preferred_element_type=F32)
        lanes = slice(j * LANE, (j + 1) * LANE)
        out_ref[:, lanes] = (xr[j].astype(F32) + modc[2] * total).astype(BF16)

    wo_recv[t] = wo_send[t]
    finish(0)
    finish(1)
    finish(2)
    relay_y(ab, r_ab, 0)
    relay_y(ab, r_ab, 1)
    relay_y(ab, r_ab, 2)
    relay_far(ab, r_ab, 0)
    relay_sides(ab, r_ab, 0)
    relay_far(ab, r_ab, 1)
    relay_sides(ab, r_ab, 1)
    relay_far(ab, r_ab, 2)
    relay_sides(ab, r_ab, 2)
    late(ab, r_ab, 0)
    mix(0)
    late(ab, r_ab, 1)
    mix(1)
    late(ab, r_ab, 2)
    mix(2)
    for copy in sends:
        copy.wait_send()


def local(frames_in, fresh, levels, reach, level_mod, w_qkv, q_gain, k_gain, w_out):
    queues = lax.axis_size("queue")
    tokens, part = fresh.shape
    model = w_qkv.shape[0]
    blocks = tokens // LANE
    vmem = pltpu.VMEM
    dma = pltpu.SemaphoreType.DMA
    any_spec = pl.BlockSpec(memory_space=pl.ANY)
    out = pl.pallas_call(
        lambda *refs: kernel(queues, *refs),
        out_shape=jax.ShapeDtypeStruct((part, tokens), BF16),
        in_specs=[pl.BlockSpec(memory_space=pltpu.HBM)] * 2 + [any_spec] * 7,
        out_specs=pl.BlockSpec(memory_space=pltpu.VMEM),
        scratch_shapes=[
            vmem((blocks, part, LANE), BF16),
            vmem((blocks, part, LANE), BF16),
            vmem((8, LANE), F32),
            vmem((16, 8, LANE), F32),
            vmem((3, part, LANE), BF16),
            vmem((3, part, 1), F32),
            vmem((3, model, LANE), BF16),
            vmem((8, 3 * HD, 2 * part), BF16),
            vmem((blocks, 16, part, LANE), BF16),
            vmem((HD, tokens), BF16),
            vmem((7, blocks, 2, HD, HD), BF16),
            vmem((8, tokens), F32),
            vmem((8, tokens), F32),
            vmem((HD, tokens), F32),
            vmem((blocks, 16, HD, LANE), BF16),
            vmem((HD, model), BF16),
            vmem((16, part, HD), BF16),
            vmem((16, part, HD), BF16),
            vmem((16, LANE), F32),
            pltpu.SMEM((1,), jnp.int32),
            pltpu.SMEM((1,), jnp.int32),
            dma((16,)),
            dma((160,)),
            dma((blocks,)),
            dma((16,)),
            dma((blocks, 16)),
            dma((7, blocks)),
            dma((blocks, 16)),
            dma((16,)),
        ],
        compiler_params=pltpu.CompilerParams(
            collective_id=0, has_side_effects=True, vmem_limit_bytes=56 * 1024 * 1024
        ),
        name="block",
    )(
        levels, reach, frames_in[0].T, fresh.T, jnp.transpose(level_mod, (1, 2, 0)),
        jnp.transpose(w_qkv, (1, 0, 2)), q_gain.reshape(1, HD), k_gain.reshape(1, HD), w_out,
    )
    return out.T[None]


def solution(mesh):
    return jax.shard_map(
        local,
        mesh=mesh,
        in_specs=(
            P("queue", None, "tensor"),
            P(None, "tensor"),
            P("queue"),
            P("queue"),
            P(None, None, "tensor"),
            P(None, None, "tensor"),
            P("tensor"),
            P("tensor"),
            P("tensor", None),
        ),
        out_specs=P("queue", None, "tensor"),
        check_vma=False,
    )
```

```python
import jax
import jax.numpy as jnp
from jax import lax
from jax.experimental import pallas as pl
from jax.experimental.pallas import tpu as pltpu
from jax.sharding import PartitionSpec as P

MESH = pl.DeviceIdType.MESH
HD = 128
EPS = 1e-06
LANE = 128
F32 = jnp.float32
BF16 = jnp.bfloat16


def kernel(
    queues, levels_ref, reach_ref, frames_ref, fresh_ref, mod_ref, w_ref, qg_ref, kg_ref, wo_ref,
    out_ref,
    xs, xr, st, stb, lm, modc, wq, wt, hb, qt, kv, m_s, l_s, o_s, ab, wo_in, wo_send, wo_recv, gains,
    level_s, reach_s, local_sem, ss, r_shift, r_stat, r_h, r_kv, r_ab, r_wo,
):
    blocks = xs.shape[0]
    part = xs.shape[1]
    width = 16 * part
    q = lax.axis_index("queue")
    t = lax.axis_index("tensor")
    z, e = q // 2, q % 2
    x, y, c = t // 4, (t // 2) % 2, t % 2
    zs = queues // 2

    def tid(dx, fy, fc):
        xx = (x + dx) % 4
        yy = (y + fy) % 2
        cc = (c + fc) % 2
        return xx * 4 + yy * 2 + cc

    def queue_id(dz, flip):
        return ((z + dz + zs) % zs) * 2 + (e + flip) % 2

    sends = []

    def send(src, dst, recv_sem, device):
        copy = pltpu.make_async_remote_copy(
            src_ref=src, dst_ref=dst, send_sem=ss.at[len(sends)], recv_sem=recv_sem,
            device_id=device, device_id_type=MESH,
        )
        copy.start()
        sends.append(copy)

    def arrived(dst, recv_sem):
        pltpu.make_async_remote_copy(
            src_ref=dst, dst_ref=dst, send_sem=ss.at[0], recv_sem=recv_sem,
            device_id=(q, tid(0, 0, 1)), device_id_type=MESH,
        ).wait_recv()

    last = q == queues - 1
    loads = []

    def load(src, dst):
        copy = pltpu.make_async_copy(src, dst, local_sem.at[len(loads)])
        loads.append(copy)
        return copy

    for j in range(blocks):
        lanes = pl.ds(j * LANE, LANE)
        from_queue = load(frames_ref.at[:, lanes], xs.at[j])
        from_noise = pltpu.make_async_copy(fresh_ref.at[:, lanes], xs.at[j], local_sem.at[j])

        @pl.when(last)
        def _():
            from_noise.start()

        @pl.when(jnp.logical_not(last))
        def _():
            from_queue.start()

    load_wo = load(wo_ref, wo_in)
    load_level = load(levels_ref, level_s)
    load_reach = load(reach_ref, reach_s)
    load_mod = load(mod_ref, lm)
    load_w = load(w_ref, wq)
    load_qg = load(qg_ref, gains.at[pl.ds(0, 1)])
    load_kg = load(kg_ref, gains.at[pl.ds(8, 1)])
    for copy in loads[blocks:]:
        copy.start()

    after = (q + 1) % queues
    before = (q + queues - 1) % queues
    barrier = pltpu.get_barrier_semaphore()
    for k in range(1, 16):
        pl.semaphore_signal(barrier, inc=1, device_id=(q, (t + k) % 16), device_id_type=MESH)
    for k in range(16):
        pl.semaphore_signal(barrier, inc=1, device_id=(after, (t + k) % 16), device_id_type=MESH)
        pl.semaphore_signal(barrier, inc=1, device_id=(before, (t + k) % 16), device_id_type=MESH)
    for dz in (1, -1):
        pl.semaphore_signal(barrier, inc=1, device_id=(queue_id(dz, 0), t), device_id_type=MESH)
    sigma = 2 * e - 1
    pl.semaphore_signal(barrier, inc=1, device_id=(queue_id(2 * sigma, 1), t), device_id_type=MESH)

    for j in range(blocks):
        loads[j].wait()
        values = xs[j].astype(F32)
        total = jnp.sum(values, axis=0, keepdims=True)
        rest = values - total * (1.0 / part)
        st[j : j + 1, :] = total
        st[blocks + j : blocks + j + 1, :] = jnp.sum(rest * rest, axis=0, keepdims=True)
    pl.semaphore_wait(barrier, 15 + 32 + 3)

    send(xs.at[0], xr.at[0], r_shift.at[0], (after, t))
    for k in range(16):
        send(st, stb.at[t], r_stat.at[t], (after, (t + k) % 16))
    for j in range(1, blocks):
        send(xs.at[j], xr.at[j], r_shift.at[j], (after, t))

    load_wo.wait()

    def turn_out(k, _):
        lanes = pl.ds(pl.multiple_of(k * 384, 128), 384)
        wo_send[pl.ds(2 * k, 2)] = wo_in[:, lanes].T.reshape(2, part, LANE)
        return 0

    lax.fori_loop(0, 8, turn_out, 0)

    def send_out(across, steps):
        for dx in steps:
            for fc in range(2):
                if across:
                    target = tid(dx, 1, fc)
                    send(wo_send.at[target], wo_recv.at[t], r_wo.at[t], (queue_id(0, fc), target))
                elif dx or fc:
                    target = tid(dx, 0, fc)
                    send(wo_send.at[target], wo_recv.at[t], r_wo.at[t], (q, target))

    send_out(False, (2, 1, 3, 0))

    load_level.wait()
    load_reach.wait()
    load_mod.wait()
    chosen = lax.broadcasted_iota(jnp.int32, (part, LANE), 1) == level_s[0]
    for k in range(3):
        modc[k] = jnp.sum(jnp.where(chosen, lm[k].astype(F32), 0.0), axis=1, keepdims=True)
    load_qg.wait()
    load_kg.wait()
    eye = lax.broadcasted_iota(jnp.int32, (HD, HD), 0) == lax.broadcasted_iota(jnp.int32, (HD, HD), 1)
    q_gain = jnp.sum(jnp.where(eye, gains[0:1, :], 0.0), axis=1, keepdims=True)
    k_gain = jnp.sum(jnp.where(eye, gains[8:9, :], 0.0), axis=1, keepdims=True)

    load_w.wait()

    def turn(chip, _):
        for k in range(3):
            for piece in range(3):
                rows = pl.ds(pl.multiple_of(chip * 384 + piece * 128, 128), 128)
                wt[chip, k * 128 : (k + 1) * 128, piece * 128 : (piece + 1) * 128] = wq[k, rows, :].T
        return 0

    lax.fori_loop(0, 8, turn, 0)

    def slot_wait(buf, sems, j, slot):
        arrived(buf.at[j, slot], sems.at[j, slot])

    def slot_send(buf, sems, j, slot, device_t):
        send(buf.at[j, slot], buf.at[j, slot], sems.at[j, slot], (q, device_t))

    other = tid(0, 0, 1)
    order = ((0, 0), (0, 1), (1, 0), (3, 0), (2, 0), (1, 1), (3, 1), (2, 1))

    def gather_own(buf, sems, j):
        for target in (tid(0, 1, 0), tid(2, 0, 0), tid(1, 0, 0), tid(3, 0, 0), other):
            slot_send(buf, sems, j, t, target)

    def relay_y(buf, sems, j):
        slot = tid(0, 1, 0)
        slot_wait(buf, sems, j, slot)
        for target in (tid(1, 0, 0), tid(3, 0, 0), other):
            slot_send(buf, sems, j, slot, target)

    def relay_far(buf, sems, j):
        slot = tid(2, 0, 0)
        slot_wait(buf, sems, j, slot)
        slot_send(buf, sems, j, slot, tid(0, 1, 0))
        slot_send(buf, sems, j, slot, other)

    def relay_chip(buf, sems, j, dx, fy):
        slot = tid(dx, fy, 0)
        slot_wait(buf, sems, j, slot)
        slot_send(buf, sems, j, slot, other)

    def relay_sides(buf, sems, j):
        relay_chip(buf, sems, j, 1, 0)
        relay_chip(buf, sems, j, 3, 0)

    def late(buf, sems, j):
        relay_chip(buf, sems, j, 1, 1)
        relay_chip(buf, sems, j, 3, 1)
        relay_chip(buf, sems, j, 2, 1)

    for k in range(16):
        slot = (t + k) % 16
        arrived(stb.at[slot], r_stat.at[slot])
    center = jnp.sum(stb[:, 0:blocks, :], axis=0) * (1.0 / width)
    offs = stb[:, 0:blocks, :] * (1.0 / part) - center[None]
    spread = jnp.sum(stb[:, blocks : 2 * blocks, :] + part * offs * offs, axis=0) * (1.0 / width)
    factor = lax.rsqrt(spread + EPS)

    def normalise(j):
        arrived(xr.at[j], r_shift.at[j])
        normed = (xr[j].astype(F32) - center[j : j + 1, :]) * factor[j : j + 1, :]
        hb[j, t] = (normed * (1.0 + modc[1]) + modc[0]).astype(BF16)
        gather_own(hb, r_h, j)

    own, s_near, s_away, o_0, o_near, o_away, o_far = range(7)

    def kv_send(j, slot, there, device):
        send(kv.at[slot, j], kv.at[there, j], r_kv.at[there, j], device)

    def kv_wait(j, slot):
        arrived(kv.at[slot, j], r_kv.at[slot, j])

    def project(j):
        def one(chip, total):
            h = hb[j, pl.ds(2 * chip, 2)].reshape(2 * part, LANE)
            return total + jnp.dot(wt[chip], h, preferred_element_type=F32)

        packed = jnp.zeros((3 * HD, LANE), F32)
        for dx, fy in order:
            slot_wait(hb, r_h, j, tid(dx, fy, 1))
            packed = one(tid(dx, fy, 0) // 2, packed)
        query, keyed, valued = packed[:HD], packed[HD : 2 * HD], packed[2 * HD :]

        def rms(values, gain):
            power = jnp.mean(values * values, axis=0, keepdims=True)
            return (values * lax.rsqrt(power + EPS) * gain).astype(BF16)

        kv[own, j, 0] = rms(keyed, k_gain).T
        kv[own, j, 1] = valued.astype(BF16)
        kv_send(j, own, o_0, (queue_id(0, 1), t))
        if j == blocks - 1:
            kv_send(j, own, o_far, (queue_id(2 * sigma, 1), t))
        kv_send(j, own, s_near, (queue_id(sigma, 0), t))
        kv_send(j, own, s_away, (queue_id(-sigma, 0), t))
        qt[:, j * LANE : (j + 1) * LANE] = rms(query, q_gain)

    def kv_relay_1(j):
        kv_wait(j, o_0)
        kv_send(j, o_0, o_near, (queue_id(-sigma, 0), t))
        kv_send(j, o_0, o_away, (queue_id(sigma, 0), t))

    def kv_relay_2(j):
        kv_wait(j, o_near)
        kv_send(j, o_near, o_far, (queue_id(-sigma, 0), t))

    normalise(0)
    normalise(1)
    relay_y(hb, r_h, 0)
    normalise(2)
    relay_far(hb, r_h, 0)
    relay_y(hb, r_h, 1)
    relay_sides(hb, r_h, 0)
    relay_far(hb, r_h, 1)
    relay_y(hb, r_h, 2)
    relay_sides(hb, r_h, 1)
    late(hb, r_h, 0)
    relay_far(hb, r_h, 2)
    project(0)
    relay_sides(hb, r_h, 2)
    late(hb, r_h, 1)
    project(1)
    kv_relay_1(0)
    late(hb, r_h, 2)
    project(2)
    kv_relay_1(1)
    kv_relay_2(0)

    f = q
    scale = HD ** (-0.5)
    m_s[...] = jnp.full(m_s.shape, -jnp.inf, F32)
    l_s[...] = jnp.zeros(l_s.shape, F32)
    o_s[...] = jnp.zeros(o_s.shape, F32)

    def attend(slot, offset, span=(0, 3)):
        lanes = slice(span[0] * LANE, span[1] * LANE)
        keys = kv[slot, :, 0].reshape(blocks * LANE, HD)
        scores = jnp.dot(keys, qt[:, lanes], preferred_element_type=F32)
        frame = f + offset
        usable = (jnp.abs(offset) <= reach_s[0]) & (frame >= 0) & (frame < queues)
        scores = scores * scale + jnp.where(usable, 0.0, -jnp.inf).astype(F32)
        m_old = m_s[0:1, lanes]
        m_new = jnp.maximum(m_old, jnp.max(scores, axis=0, keepdims=True))
        weights = jnp.exp(scores - m_new)
        fade = jnp.exp(m_old - m_new)
        l_s[0:1, lanes] = l_s[0:1, lanes] * fade + jnp.sum(weights, axis=0, keepdims=True)
        m_s[0:1, lanes] = m_new
        half = weights.astype(BF16)
        values = jnp.concatenate([kv[slot, j, 1] for j in range(blocks)], axis=1)
        o_s[:, lanes] = o_s[:, lanes] * fade + jnp.dot(values, half, preferred_element_type=F32)

    attend(own, 0)
    kv_relay_1(2)
    kv_relay_2(1)
    send_out(True, (2, 1, 3, 0))
    attend(o_0, -sigma)
    for slot, offset in ((s_near, -2 * sigma), (s_away, 2 * sigma), (o_far, 3 * sigma)):
        for j in range(blocks):
            kv_wait(j, slot)
        attend(slot, offset)
    kv_wait(blocks - 1, o_near)
    attend(o_near, sigma)
    for j in range(blocks):
        kv_wait(j, o_away)

    def finish(j):
        attend(o_away, -3 * sigma, (j, j + 1))
        lanes = slice(j * LANE, (j + 1) * LANE)
        ab[j, t] = (o_s[:, lanes] / l_s[0:1, lanes]).astype(BF16)
        gather_own(ab, r_ab, j)

    def out_wait(dx, fy, fc):
        if dx or fy or fc:
            source = tid(dx, fy, fc)
            arrived(wo_recv.at[source], r_wo.at[source])

    def mix(j):
        total = jnp.zeros((part, LANE), F32)
        for dx, fy in order:
            slot_wait(ab, r_ab, j, tid(dx, fy, 1))
            if j == 0:
                out_wait(dx, fy, 0)
                out_wait(dx, fy, 1)
            k = tid(dx, fy, 0) // 2
            weights = jnp.concatenate([wo_recv[2 * k], wo_recv[2 * k + 1]], axis=1)
            heads = ab[j, pl.ds(2 * k, 2)].reshape(2 * HD, LANE)
            total = total + jnp.dot(weights, heads, preferred_element_type=F32)
        lanes = slice(j * LANE, (j + 1) * LANE)
        out_ref[:, lanes] = (xr[j].astype(F32) + modc[2] * total).astype(BF16)

    wo_recv[t] = wo_send[t]
    finish(0)
    finish(1)
    finish(2)
    relay_y(ab, r_ab, 0)
    relay_y(ab, r_ab, 1)
    relay_y(ab, r_ab, 2)
    relay_far(ab, r_ab, 0)
    relay_sides(ab, r_ab, 0)
    relay_far(ab, r_ab, 1)
    relay_sides(ab, r_ab, 1)
    relay_far(ab, r_ab, 2)
    relay_sides(ab, r_ab, 2)
    late(ab, r_ab, 0)
    mix(0)
    late(ab, r_ab, 1)
    mix(1)
    late(ab, r_ab, 2)
    mix(2)
    for copy in sends:
        copy.wait_send()


def local(frames_in, fresh, levels, reach, level_mod, w_qkv, q_gain, k_gain, w_out):
    queues = lax.axis_size("queue")
    tokens, part = fresh.shape
    model = w_qkv.shape[0]
    blocks = tokens // LANE
    vmem = pltpu.VMEM
    dma = pltpu.SemaphoreType.DMA
    any_spec = pl.BlockSpec(memory_space=pl.ANY)
    out = pl.pallas_call(
        lambda *refs: kernel(queues, *refs),
        out_shape=pltpu.VMEM((part, tokens), BF16),
        in_specs=[pl.BlockSpec(memory_space=pltpu.HBM)] * 2 + [any_spec] * 7,
        out_specs=pl.BlockSpec(memory_space=pltpu.VMEM),
        scratch_shapes=[
            vmem((blocks, part, LANE), BF16),
            vmem((blocks, part, LANE), BF16),
            vmem((8, LANE), F32),
            vmem((16, 8, LANE), F32),
            vmem((3, part, LANE), BF16),
            vmem((3, part, 1), F32),
            vmem((3, model, LANE), BF16),
            vmem((8, 3 * HD, 2 * part), BF16),
            vmem((blocks, 16, part, LANE), BF16),
            vmem((HD, tokens), BF16),
            vmem((7, blocks, 2, HD, HD), BF16),
            vmem((8, tokens), F32),
            vmem((8, tokens), F32),
            vmem((HD, tokens), F32),
            vmem((blocks, 16, HD, LANE), BF16),
            vmem((HD, model), BF16),
            vmem((16, part, HD), BF16),
            vmem((16, part, HD), BF16),
            vmem((16, LANE), F32),
            pltpu.SMEM((1,), jnp.int32),
            pltpu.SMEM((1,), jnp.int32),
            dma((16,)),
            dma((160,)),
            dma((blocks,)),
            dma((16,)),
            dma((blocks, 16)),
            dma((7, blocks)),
            dma((blocks, 16)),
            dma((16,)),
        ],
        compiler_params=pltpu.CompilerParams(
            collective_id=0, has_side_effects=True, vmem_limit_bytes=56 * 1024 * 1024
        ),
        name="block",
    )(
        levels, reach, frames_in[0].T, fresh.T, jnp.transpose(level_mod, (1, 2, 0)),
        jnp.transpose(w_qkv, (1, 0, 2)), q_gain.reshape(1, HD), k_gain.reshape(1, HD), w_out,
    )
    return out.T[None]


def solution(mesh):
    return jax.shard_map(
        local,
        mesh=mesh,
        in_specs=(
            P("queue", None, "tensor"),
            P(None, "tensor"),
            P("queue"),
            P("queue"),
            P(None, None, "tensor"),
            P(None, None, "tensor"),
            P("tensor"),
            P("tensor"),
            P("tensor", None),
        ),
        out_specs=P("queue", None, "tensor"),
        check_vma=False,
    )
```

```python
import jax
import jax.numpy as jnp
from jax import lax
from jax.experimental import pallas as pl
from jax.experimental.pallas import tpu as pltpu
from jax.sharding import PartitionSpec as P

MESH = pl.DeviceIdType.MESH
HD = 128
EPS = 1e-06
LANE = 128
F32 = jnp.float32
BF16 = jnp.bfloat16


def kernel(
    queues, levels_ref, reach_ref, frames_ref, fresh_ref, mod_ref, w_ref, qg_ref, kg_ref, wo_ref,
    out_ref,
    xs, xr, st, stb, lm, modc, wq, wt, hb, qt, kv, m_s, l_s, o_s, ab, wo_in, wo_send, wo_recv, gains,
    level_s, reach_s, local_sem, ss, r_shift, r_stat, r_h, r_kv, r_ab, r_wo,
):
    blocks = xs.shape[0]
    part = xs.shape[1]
    width = 16 * part
    q = lax.axis_index("queue")
    t = lax.axis_index("tensor")
    z, e = q // 2, q % 2
    x, y, c = t // 4, (t // 2) % 2, t % 2
    zs = queues // 2

    def tid(dx, fy, fc):
        xx = (x + dx) % 4
        yy = (y + fy) % 2
        cc = (c + fc) % 2
        return xx * 4 + yy * 2 + cc

    def queue_id(dz, flip):
        return ((z + dz + zs) % zs) * 2 + (e + flip) % 2

    sends = []

    def send(src, dst, recv_sem, device):
        copy = pltpu.make_async_remote_copy(
            src_ref=src, dst_ref=dst, send_sem=ss.at[len(sends)], recv_sem=recv_sem,
            device_id=device, device_id_type=MESH,
        )
        copy.start()
        sends.append(copy)

    def arrived(dst, recv_sem):
        pltpu.make_async_remote_copy(
            src_ref=dst, dst_ref=dst, send_sem=ss.at[0], recv_sem=recv_sem,
            device_id=(q, tid(0, 0, 1)), device_id_type=MESH,
        ).wait_recv()

    last = q == queues - 1
    loads = []

    def load(src, dst):
        copy = pltpu.make_async_copy(src, dst, local_sem.at[len(loads)])
        loads.append(copy)
        return copy

    for j in range(blocks):
        lanes = pl.ds(j * LANE, LANE)
        from_queue = load(frames_ref.at[:, lanes], xs.at[j])
        from_noise = pltpu.make_async_copy(fresh_ref.at[:, lanes], xs.at[j], local_sem.at[j])

        @pl.when(last)
        def _():
            from_noise.start()

        @pl.when(jnp.logical_not(last))
        def _():
            from_queue.start()

    load_wo = load(wo_ref, wo_in)
    load_level = load(levels_ref, level_s)
    load_reach = load(reach_ref, reach_s)
    load_mod = load(mod_ref, lm)
    load_w = load(w_ref, wq)
    load_qg = load(qg_ref, gains.at[pl.ds(0, 1)])
    load_kg = load(kg_ref, gains.at[pl.ds(8, 1)])
    for copy in loads[blocks:]:
        copy.start()

    after = (q + 1) % queues
    before = (q + queues - 1) % queues
    barrier = pltpu.get_barrier_semaphore()
    for k in range(1, 16):
        pl.semaphore_signal(barrier, inc=1, device_id=(q, (t + k) % 16), device_id_type=MESH)
    for k in range(16):
        pl.semaphore_signal(barrier, inc=1, device_id=(after, (t + k) % 16), device_id_type=MESH)
        pl.semaphore_signal(barrier, inc=1, device_id=(before, (t + k) % 16), device_id_type=MESH)
    for dz in (1, -1):
        pl.semaphore_signal(barrier, inc=1, device_id=(queue_id(dz, 0), t), device_id_type=MESH)
    sigma = 2 * e - 1
    pl.semaphore_signal(barrier, inc=1, device_id=(queue_id(2 * sigma, 1), t), device_id_type=MESH)

    for j in range(blocks):
        loads[j].wait()
        values = xs[j].astype(F32)
        total = jnp.sum(values, axis=0, keepdims=True)
        rest = values - total * (1.0 / part)
        st[j : j + 1, :] = total
        st[blocks + j : blocks + j + 1, :] = jnp.sum(rest * rest, axis=0, keepdims=True)
    pl.semaphore_wait(barrier, 15 + 32 + 3)

    for k in range(16):
        send(st, stb.at[t], r_stat.at[t], (after, (t + k) % 16))
    send(xs.at[0], xr.at[0], r_shift.at[0], (after, t))
    for j in range(1, blocks):
        send(xs.at[j], xr.at[j], r_shift.at[j], (after, t))

    load_wo.wait()

    def turn_out(k, _):
        lanes = pl.ds(pl.multiple_of(k * 384, 128), 384)
        wo_send[pl.ds(2 * k, 2)] = wo_in[:, lanes].T.reshape(2, part, LANE)
        return 0

    lax.fori_loop(0, 8, turn_out, 0)

    def send_out(across, steps):
        for dx in steps:
            for fc in range(2):
                if across:
                    target = tid(dx, 1, fc)
                    send(wo_send.at[target], wo_recv.at[t], r_wo.at[t], (queue_id(0, fc), target))
                elif dx or fc:
                    target = tid(dx, 0, fc)
                    send(wo_send.at[target], wo_recv.at[t], r_wo.at[t], (q, target))

    send_out(False, (2, 1, 3, 0))

    load_level.wait()
    load_reach.wait()
    load_mod.wait()
    chosen = lax.broadcasted_iota(jnp.int32, (part, LANE), 1) == level_s[0]
    for k in range(3):
        modc[k] = jnp.sum(jnp.where(chosen, lm[k].astype(F32), 0.0), axis=1, keepdims=True)
    load_qg.wait()
    load_kg.wait()
    eye = lax.broadcasted_iota(jnp.int32, (HD, HD), 0) == lax.broadcasted_iota(jnp.int32, (HD, HD), 1)
    q_gain = jnp.sum(jnp.where(eye, gains[0:1, :], 0.0), axis=1, keepdims=True)
    k_gain = jnp.sum(jnp.where(eye, gains[8:9, :], 0.0), axis=1, keepdims=True)

    load_w.wait()

    def turn(chip, _):
        for k in range(3):
            for piece in range(3):
                rows = pl.ds(pl.multiple_of(chip * 384 + piece * 128, 128), 128)
                wt[chip, k * 128 : (k + 1) * 128, piece * 128 : (piece + 1) * 128] = wq[k, rows, :].T
        return 0

    lax.fori_loop(0, 8, turn, 0)

    def slot_wait(buf, sems, j, slot):
        arrived(buf.at[j, slot], sems.at[j, slot])

    def slot_send(buf, sems, j, slot, device_t):
        send(buf.at[j, slot], buf.at[j, slot], sems.at[j, slot], (q, device_t))

    other = tid(0, 0, 1)
    order = ((0, 0), (0, 1), (1, 0), (3, 0), (2, 0), (1, 1), (3, 1), (2, 1))

    def gather_own(buf, sems, j):
        for target in (tid(0, 1, 0), tid(2, 0, 0), tid(1, 0, 0), tid(3, 0, 0), other):
            slot_send(buf, sems, j, t, target)

    def relay_y(buf, sems, j):
        slot = tid(0, 1, 0)
        slot_wait(buf, sems, j, slot)
        for target in (tid(1, 0, 0), tid(3, 0, 0), other):
            slot_send(buf, sems, j, slot, target)

    def relay_far(buf, sems, j):
        slot = tid(2, 0, 0)
        slot_wait(buf, sems, j, slot)
        slot_send(buf, sems, j, slot, tid(0, 1, 0))
        slot_send(buf, sems, j, slot, other)

    def relay_chip(buf, sems, j, dx, fy):
        slot = tid(dx, fy, 0)
        slot_wait(buf, sems, j, slot)
        slot_send(buf, sems, j, slot, other)

    def relay_sides(buf, sems, j):
        relay_chip(buf, sems, j, 1, 0)
        relay_chip(buf, sems, j, 3, 0)

    def late(buf, sems, j):
        relay_chip(buf, sems, j, 1, 1)
        relay_chip(buf, sems, j, 3, 1)
        relay_chip(buf, sems, j, 2, 1)

    for k in range(16):
        slot = (t + k) % 16
        arrived(stb.at[slot], r_stat.at[slot])
    center = jnp.sum(stb[:, 0:blocks, :], axis=0) * (1.0 / width)
    offs = stb[:, 0:blocks, :] * (1.0 / part) - center[None]
    spread = jnp.sum(stb[:, blocks : 2 * blocks, :] + part * offs * offs, axis=0) * (1.0 / width)
    factor = lax.rsqrt(spread + EPS)

    def normalise(j):
        arrived(xr.at[j], r_shift.at[j])
        normed = (xr[j].astype(F32) - center[j : j + 1, :]) * factor[j : j + 1, :]
        hb[j, t] = (normed * (1.0 + modc[1]) + modc[0]).astype(BF16)
        gather_own(hb, r_h, j)

    own, s_near, s_away, o_0, o_near, o_away, o_far = range(7)

    def kv_send(j, slot, there, device):
        send(kv.at[slot, j], kv.at[there, j], r_kv.at[there, j], device)

    def kv_wait(j, slot):
        arrived(kv.at[slot, j], r_kv.at[slot, j])

    def project(j):
        def one(chip, total):
            h = hb[j, pl.ds(2 * chip, 2)].reshape(2 * part, LANE)
            return total + jnp.dot(wt[chip], h, preferred_element_type=F32)

        packed = jnp.zeros((3 * HD, LANE), F32)
        for dx, fy in order:
            slot_wait(hb, r_h, j, tid(dx, fy, 1))
            packed = one(tid(dx, fy, 0) // 2, packed)
        query, keyed, valued = packed[:HD], packed[HD : 2 * HD], packed[2 * HD :]

        def rms(values, gain):
            power = jnp.mean(values * values, axis=0, keepdims=True)
            return (values * lax.rsqrt(power + EPS) * gain).astype(BF16)

        kv[own, j, 0] = rms(keyed, k_gain).T
        kv[own, j, 1] = valued.astype(BF16)
        kv_send(j, own, o_0, (queue_id(0, 1), t))
        if j == blocks - 1:
            kv_send(j, own, o_far, (queue_id(2 * sigma, 1), t))
        kv_send(j, own, s_near, (queue_id(sigma, 0), t))
        kv_send(j, own, s_away, (queue_id(-sigma, 0), t))
        qt[:, j * LANE : (j + 1) * LANE] = rms(query, q_gain)

    def kv_relay_1(j):
        kv_wait(j, o_0)
        kv_send(j, o_0, o_near, (queue_id(-sigma, 0), t))
        kv_send(j, o_0, o_away, (queue_id(sigma, 0), t))

    def kv_relay_2(j):
        kv_wait(j, o_near)
        kv_send(j, o_near, o_far, (queue_id(-sigma, 0), t))

    normalise(0)
    normalise(1)
    relay_y(hb, r_h, 0)
    normalise(2)
    relay_far(hb, r_h, 0)
    relay_y(hb, r_h, 1)
    relay_sides(hb, r_h, 0)
    relay_far(hb, r_h, 1)
    relay_y(hb, r_h, 2)
    relay_sides(hb, r_h, 1)
    late(hb, r_h, 0)
    relay_far(hb, r_h, 2)
    project(0)
    relay_sides(hb, r_h, 2)
    late(hb, r_h, 1)
    project(1)
    late(hb, r_h, 2)
    kv_relay_1(0)
    project(2)
    kv_relay_1(1)
    kv_relay_2(0)

    f = q
    scale = HD ** (-0.5)
    m_s[...] = jnp.full(m_s.shape, -jnp.inf, F32)
    l_s[...] = jnp.zeros(l_s.shape, F32)
    o_s[...] = jnp.zeros(o_s.shape, F32)

    def attend(slot, offset, span=(0, 3)):
        lanes = slice(span[0] * LANE, span[1] * LANE)
        keys = kv[slot, :, 0].reshape(blocks * LANE, HD)
        scores = jnp.dot(keys, qt[:, lanes], preferred_element_type=F32)
        frame = f + offset
        usable = (jnp.abs(offset) <= reach_s[0]) & (frame >= 0) & (frame < queues)
        scores = scores * scale + jnp.where(usable, 0.0, -jnp.inf).astype(F32)
        m_old = m_s[0:1, lanes]
        m_new = jnp.maximum(m_old, jnp.max(scores, axis=0, keepdims=True))
        weights = jnp.exp(scores - m_new)
        fade = jnp.exp(m_old - m_new)
        l_s[0:1, lanes] = l_s[0:1, lanes] * fade + jnp.sum(weights, axis=0, keepdims=True)
        m_s[0:1, lanes] = m_new
        half = weights.astype(BF16)
        values = jnp.concatenate([kv[slot, j, 1] for j in range(blocks)], axis=1)
        o_s[:, lanes] = o_s[:, lanes] * fade + jnp.dot(values, half, preferred_element_type=F32)

    attend(own, 0)
    kv_relay_1(2)
    kv_relay_2(1)
    send_out(True, (2, 1, 3, 0))
    attend(o_0, -sigma)
    for slot, offset in ((s_near, -2 * sigma), (s_away, 2 * sigma), (o_far, 3 * sigma)):
        for j in range(blocks):
            kv_wait(j, slot)
        attend(slot, offset)
    kv_wait(blocks - 1, o_near)
    attend(o_near, sigma)
    for j in range(blocks):
        kv_wait(j, o_away)

    def finish(j):
        attend(o_away, -3 * sigma, (j, j + 1))
        lanes = slice(j * LANE, (j + 1) * LANE)
        ab[j, t] = (o_s[:, lanes] / l_s[0:1, lanes]).astype(BF16)
        gather_own(ab, r_ab, j)

    def out_wait(dx, fy, fc):
        if dx or fy or fc:
            source = tid(dx, fy, fc)
            arrived(wo_recv.at[source], r_wo.at[source])

    def mix(j):
        total = jnp.zeros((part, LANE), F32)
        for dx, fy in order:
            slot_wait(ab, r_ab, j, tid(dx, fy, 1))
            if j == 0:
                out_wait(dx, fy, 0)
                out_wait(dx, fy, 1)
            k = tid(dx, fy, 0) // 2
            weights = jnp.concatenate([wo_recv[2 * k], wo_recv[2 * k + 1]], axis=1)
            heads = ab[j, pl.ds(2 * k, 2)].reshape(2 * HD, LANE)
            total = total + jnp.dot(weights, heads, preferred_element_type=F32)
        lanes = slice(j * LANE, (j + 1) * LANE)
        out_ref[:, lanes] = (xr[j].astype(F32) + modc[2] * total).astype(BF16)

    wo_recv[t] = wo_send[t]
    finish(0)
    finish(1)
    finish(2)
    relay_y(ab, r_ab, 0)
    relay_y(ab, r_ab, 1)
    relay_y(ab, r_ab, 2)
    relay_far(ab, r_ab, 0)
    relay_sides(ab, r_ab, 0)
    relay_far(ab, r_ab, 1)
    relay_sides(ab, r_ab, 1)
    relay_far(ab, r_ab, 2)
    relay_sides(ab, r_ab, 2)
    late(ab, r_ab, 0)
    mix(0)
    late(ab, r_ab, 1)
    mix(1)
    late(ab, r_ab, 2)
    mix(2)
    for copy in sends:
        copy.wait_send()


def local(frames_in, fresh, levels, reach, level_mod, w_qkv, q_gain, k_gain, w_out):
    queues = lax.axis_size("queue")
    tokens, part = fresh.shape
    model = w_qkv.shape[0]
    blocks = tokens // LANE
    vmem = pltpu.VMEM
    dma = pltpu.SemaphoreType.DMA
    any_spec = pl.BlockSpec(memory_space=pl.ANY)
    out = pl.pallas_call(
        lambda *refs: kernel(queues, *refs),
        out_shape=pltpu.VMEM((part, tokens), BF16),
        in_specs=[pl.BlockSpec(memory_space=pltpu.HBM)] * 2 + [any_spec] * 7,
        out_specs=pl.BlockSpec(memory_space=pltpu.VMEM),
        scratch_shapes=[
            vmem((blocks, part, LANE), BF16),
            vmem((blocks, part, LANE), BF16),
            vmem((8, LANE), F32),
            vmem((16, 8, LANE), F32),
            vmem((3, part, LANE), BF16),
            vmem((3, part, 1), F32),
            vmem((3, model, LANE), BF16),
            vmem((8, 3 * HD, 2 * part), BF16),
            vmem((blocks, 16, part, LANE), BF16),
            vmem((HD, tokens), BF16),
            vmem((7, blocks, 2, HD, HD), BF16),
            vmem((8, tokens), F32),
            vmem((8, tokens), F32),
            vmem((HD, tokens), F32),
            vmem((blocks, 16, HD, LANE), BF16),
            vmem((HD, model), BF16),
            vmem((16, part, HD), BF16),
            vmem((16, part, HD), BF16),
            vmem((16, LANE), F32),
            pltpu.SMEM((1,), jnp.int32),
            pltpu.SMEM((1,), jnp.int32),
            dma((16,)),
            dma((160,)),
            dma((blocks,)),
            dma((16,)),
            dma((blocks, 16)),
            dma((7, blocks)),
            dma((blocks, 16)),
            dma((16,)),
        ],
        compiler_params=pltpu.CompilerParams(
            collective_id=0, has_side_effects=True, vmem_limit_bytes=56 * 1024 * 1024
        ),
        name="block",
    )(
        levels, reach, frames_in[0].T, fresh.T, jnp.transpose(level_mod, (1, 2, 0)),
        jnp.transpose(w_qkv, (1, 0, 2)), q_gain.reshape(1, HD), k_gain.reshape(1, HD), w_out,
    )
    return out.T[None]


def solution(mesh):
    return jax.shard_map(
        local,
        mesh=mesh,
        in_specs=(
            P("queue", None, "tensor"),
            P(None, "tensor"),
            P("queue"),
            P("queue"),
            P(None, None, "tensor"),
            P(None, None, "tensor"),
            P("tensor"),
            P("tensor"),
            P("tensor", None),
        ),
        out_specs=P("queue", None, "tensor"),
        check_vma=False,
    )
```

```python
import jax
import jax.numpy as jnp
from jax import lax
from jax.experimental import pallas as pl
from jax.experimental.pallas import tpu as pltpu
from jax.sharding import PartitionSpec as P

MESH = pl.DeviceIdType.MESH
HD = 128
EPS = 1e-06
LANE = 128
F32 = jnp.float32
BF16 = jnp.bfloat16


def kernel(
    queues, levels_ref, reach_ref, frames_ref, fresh_ref, mod_ref, w_ref, qg_ref, kg_ref, wo_ref,
    out_ref,
    xs, xr, st, stb, lm, modc, wq, wt, hb, qt, kv, m_s, l_s, o_s, ab, wo_in, wo_send, wo_recv, gains,
    level_s, reach_s, local_sem, ss, r_shift, r_stat, r_h, r_kv, r_ab, r_wo,
):
    blocks = xs.shape[0]
    part = xs.shape[1]
    width = 16 * part
    q = lax.axis_index("queue")
    t = lax.axis_index("tensor")
    z, e = q // 2, q % 2
    x, y, c = t // 4, (t // 2) % 2, t % 2
    zs = queues // 2

    def tid(dx, fy, fc):
        xx = (x + dx) % 4
        yy = (y + fy) % 2
        cc = (c + fc) % 2
        return xx * 4 + yy * 2 + cc

    def queue_id(dz, flip):
        return ((z + dz + zs) % zs) * 2 + (e + flip) % 2

    sends = []

    def send(src, dst, recv_sem, device):
        copy = pltpu.make_async_remote_copy(
            src_ref=src, dst_ref=dst, send_sem=ss.at[len(sends)], recv_sem=recv_sem,
            device_id=device, device_id_type=MESH,
        )
        copy.start()
        sends.append(copy)

    def arrived(dst, recv_sem):
        pltpu.make_async_remote_copy(
            src_ref=dst, dst_ref=dst, send_sem=ss.at[0], recv_sem=recv_sem,
            device_id=(q, tid(0, 0, 1)), device_id_type=MESH,
        ).wait_recv()

    last = q == queues - 1
    loads = []

    def load(src, dst):
        copy = pltpu.make_async_copy(src, dst, local_sem.at[len(loads)])
        loads.append(copy)
        return copy

    for j in range(blocks):
        lanes = pl.ds(j * LANE, LANE)
        from_queue = load(frames_ref.at[:, lanes], xs.at[j])
        from_noise = pltpu.make_async_copy(fresh_ref.at[:, lanes], xs.at[j], local_sem.at[j])

        @pl.when(last)
        def _():
            from_noise.start()

        @pl.when(jnp.logical_not(last))
        def _():
            from_queue.start()

    load_wo = load(wo_ref, wo_in)
    load_level = load(levels_ref, level_s)
    load_reach = load(reach_ref, reach_s)
    load_mod = load(mod_ref, lm)
    load_w = load(w_ref, wq)
    load_qg = load(qg_ref, gains.at[pl.ds(0, 1)])
    load_kg = load(kg_ref, gains.at[pl.ds(8, 1)])
    for copy in loads[blocks:]:
        copy.start()

    after = (q + 1) % queues
    before = (q + queues - 1) % queues
    barrier = pltpu.get_barrier_semaphore()
    for k in range(1, 16):
        pl.semaphore_signal(barrier, inc=1, device_id=(q, (t + k) % 16), device_id_type=MESH)
    for k in range(16):
        pl.semaphore_signal(barrier, inc=1, device_id=(after, (t + k) % 16), device_id_type=MESH)
        pl.semaphore_signal(barrier, inc=1, device_id=(before, (t + k) % 16), device_id_type=MESH)
    for dz in (1, -1):
        pl.semaphore_signal(barrier, inc=1, device_id=(queue_id(dz, 0), t), device_id_type=MESH)
    sigma = 2 * e - 1
    pl.semaphore_signal(barrier, inc=1, device_id=(queue_id(2 * sigma, 1), t), device_id_type=MESH)

    for j in range(blocks):
        loads[j].wait()
        values = xs[j].astype(F32)
        total = jnp.sum(values, axis=0, keepdims=True)
        rest = values - total * (1.0 / part)
        st[j : j + 1, :] = total
        st[blocks + j : blocks + j + 1, :] = jnp.sum(rest * rest, axis=0, keepdims=True)
    pl.semaphore_wait(barrier, 15 + 32 + 3)

    for k in range(16):
        send(st, stb.at[t], r_stat.at[t], (after, (t + k) % 16))
    send(xs.at[0], xr.at[0], r_shift.at[0], (after, t))
    for j in range(1, blocks):
        send(xs.at[j], xr.at[j], r_shift.at[j], (after, t))

    load_wo.wait()

    def turn_out(k, _):
        lanes = pl.ds(pl.multiple_of(k * 384, 128), 384)
        wo_send[pl.ds(2 * k, 2)] = wo_in[:, lanes].T.reshape(2, part, LANE)
        return 0

    lax.fori_loop(0, 8, turn_out, 0)

    def send_out(across, steps):
        for dx in steps:
            for fc in range(2):
                if across:
                    target = tid(dx, 1, fc)
                    send(wo_send.at[target], wo_recv.at[t], r_wo.at[t], (queue_id(0, fc), target))
                elif dx or fc:
                    target = tid(dx, 0, fc)
                    send(wo_send.at[target], wo_recv.at[t], r_wo.at[t], (q, target))

    send_out(False, (2, 1, 3, 0))

    load_level.wait()
    load_reach.wait()
    load_mod.wait()
    chosen = lax.broadcasted_iota(jnp.int32, (part, LANE), 1) == level_s[0]
    for k in range(3):
        modc[k] = jnp.sum(jnp.where(chosen, lm[k].astype(F32), 0.0), axis=1, keepdims=True)
    load_qg.wait()
    load_kg.wait()
    eye = lax.broadcasted_iota(jnp.int32, (HD, HD), 0) == lax.broadcasted_iota(jnp.int32, (HD, HD), 1)
    q_gain = jnp.sum(jnp.where(eye, gains[0:1, :], 0.0), axis=1, keepdims=True)
    k_gain = jnp.sum(jnp.where(eye, gains[8:9, :], 0.0), axis=1, keepdims=True)

    load_w.wait()

    def turn(chip, _):
        for k in range(3):
            for piece in range(3):
                rows = pl.ds(pl.multiple_of(chip * 384 + piece * 128, 128), 128)
                wt[chip, k * 128 : (k + 1) * 128, piece * 128 : (piece + 1) * 128] = wq[k, rows, :].T
        return 0

    lax.fori_loop(0, 8, turn, 0)

    def slot_wait(buf, sems, j, slot):
        arrived(buf.at[j, slot], sems.at[j, slot])

    def slot_send(buf, sems, j, slot, device_t):
        send(buf.at[j, slot], buf.at[j, slot], sems.at[j, slot], (q, device_t))

    other = tid(0, 0, 1)
    order = ((0, 0), (0, 1), (1, 0), (3, 0), (2, 0), (1, 1), (3, 1), (2, 1))

    def gather_own(buf, sems, j):
        for target in (tid(0, 1, 0), tid(2, 0, 0), tid(1, 0, 0), tid(3, 0, 0), other):
            slot_send(buf, sems, j, t, target)

    def relay_y(buf, sems, j):
        slot = tid(0, 1, 0)
        slot_wait(buf, sems, j, slot)
        for target in (tid(1, 0, 0), tid(3, 0, 0), other):
            slot_send(buf, sems, j, slot, target)

    def relay_far(buf, sems, j):
        slot = tid(2, 0, 0)
        slot_wait(buf, sems, j, slot)
        slot_send(buf, sems, j, slot, tid(0, 1, 0))
        slot_send(buf, sems, j, slot, other)

    def relay_chip(buf, sems, j, dx, fy):
        slot = tid(dx, fy, 0)
        slot_wait(buf, sems, j, slot)
        slot_send(buf, sems, j, slot, other)

    def relay_sides(buf, sems, j):
        relay_chip(buf, sems, j, 1, 0)
        relay_chip(buf, sems, j, 3, 0)

    def late(buf, sems, j):
        relay_chip(buf, sems, j, 1, 1)
        relay_chip(buf, sems, j, 3, 1)
        relay_chip(buf, sems, j, 2, 1)

    for k in range(16):
        slot = (t + k) % 16
        arrived(stb.at[slot], r_stat.at[slot])
    center = jnp.sum(stb[:, 0:blocks, :], axis=0) * (1.0 / width)
    offs = stb[:, 0:blocks, :] * (1.0 / part) - center[None]
    spread = jnp.sum(stb[:, blocks : 2 * blocks, :] + part * offs * offs, axis=0) * (1.0 / width)
    factor = lax.rsqrt(spread + EPS)

    def normalise(j):
        arrived(xr.at[j], r_shift.at[j])
        normed = (xr[j].astype(F32) - center[j : j + 1, :]) * factor[j : j + 1, :]
        hb[j, t] = (normed * (1.0 + modc[1]) + modc[0]).astype(BF16)
        gather_own(hb, r_h, j)

    own, s_near, s_away, o_0, o_near, o_away, o_far = range(7)

    def kv_send(j, slot, there, device):
        send(kv.at[slot, j], kv.at[there, j], r_kv.at[there, j], device)

    def kv_wait(j, slot):
        arrived(kv.at[slot, j], r_kv.at[slot, j])

    def project(j):
        def one(chip, total):
            h = hb[j, pl.ds(2 * chip, 2)].reshape(2 * part, LANE)
            return total + jnp.dot(wt[chip], h, preferred_element_type=F32)

        packed = jnp.zeros((3 * HD, LANE), F32)
        for dx, fy in order:
            slot_wait(hb, r_h, j, tid(dx, fy, 1))
            packed = one(tid(dx, fy, 0) // 2, packed)
        query, keyed, valued = packed[:HD], packed[HD : 2 * HD], packed[2 * HD :]

        def rms(values, gain):
            power = jnp.mean(values * values, axis=0, keepdims=True)
            return (values * lax.rsqrt(power + EPS) * gain).astype(BF16)

        kv[own, j, 0] = rms(keyed, k_gain).T
        kv[own, j, 1] = valued.astype(BF16)
        kv_send(j, own, o_0, (queue_id(0, 1), t))
        if j == blocks - 1:
            kv_send(j, own, o_far, (queue_id(2 * sigma, 1), t))
        kv_send(j, own, s_near, (queue_id(sigma, 0), t))
        kv_send(j, own, s_away, (queue_id(-sigma, 0), t))
        qt[:, j * LANE : (j + 1) * LANE] = rms(query, q_gain)

    def kv_relay_1(j):
        kv_wait(j, o_0)
        kv_send(j, o_0, o_near, (queue_id(-sigma, 0), t))
        kv_send(j, o_0, o_away, (queue_id(sigma, 0), t))

    def kv_relay_2(j):
        kv_wait(j, o_near)
        kv_send(j, o_near, o_far, (queue_id(-sigma, 0), t))

    normalise(0)
    normalise(1)
    relay_y(hb, r_h, 0)
    normalise(2)
    relay_far(hb, r_h, 0)
    relay_y(hb, r_h, 1)
    relay_sides(hb, r_h, 0)
    relay_far(hb, r_h, 1)
    relay_y(hb, r_h, 2)
    relay_sides(hb, r_h, 1)
    late(hb, r_h, 0)
    relay_far(hb, r_h, 2)
    project(0)
    relay_sides(hb, r_h, 2)
    late(hb, r_h, 1)
    project(1)
    late(hb, r_h, 2)
    kv_relay_1(0)
    project(2)

    f = q
    scale = HD ** (-0.5)
    m_s[...] = jnp.full(m_s.shape, -jnp.inf, F32)
    l_s[...] = jnp.zeros(l_s.shape, F32)
    o_s[...] = jnp.zeros(o_s.shape, F32)

    def attend(slot, offset, span=(0, 3)):
        lanes = slice(span[0] * LANE, span[1] * LANE)
        keys = kv[slot, :, 0].reshape(blocks * LANE, HD)
        scores = jnp.dot(keys, qt[:, lanes], preferred_element_type=F32)
        frame = f + offset
        usable = (jnp.abs(offset) <= reach_s[0]) & (frame >= 0) & (frame < queues)
        scores = scores * scale + jnp.where(usable, 0.0, -jnp.inf).astype(F32)
        m_old = m_s[0:1, lanes]
        m_new = jnp.maximum(m_old, jnp.max(scores, axis=0, keepdims=True))
        weights = jnp.exp(scores - m_new)
        fade = jnp.exp(m_old - m_new)
        l_s[0:1, lanes] = l_s[0:1, lanes] * fade + jnp.sum(weights, axis=0, keepdims=True)
        m_s[0:1, lanes] = m_new
        half = weights.astype(BF16)
        values = jnp.concatenate([kv[slot, j, 1] for j in range(blocks)], axis=1)
        o_s[:, lanes] = o_s[:, lanes] * fade + jnp.dot(values, half, preferred_element_type=F32)

    attend(own, 0)
    kv_relay_1(1)
    kv_relay_2(0)
    kv_relay_1(2)
    kv_relay_2(1)
    send_out(True, (2, 1, 3, 0))
    attend(o_0, -sigma)
    for slot, offset in ((s_near, -2 * sigma), (s_away, 2 * sigma), (o_far, 3 * sigma)):
        for j in range(blocks):
            kv_wait(j, slot)
        attend(slot, offset)
    kv_wait(blocks - 1, o_near)
    attend(o_near, sigma)
    for j in range(blocks):
        kv_wait(j, o_away)

    def finish(j):
        attend(o_away, -3 * sigma, (j, j + 1))
        lanes = slice(j * LANE, (j + 1) * LANE)
        ab[j, t] = (o_s[:, lanes] / l_s[0:1, lanes]).astype(BF16)
        gather_own(ab, r_ab, j)

    def out_wait(dx, fy, fc):
        if dx or fy or fc:
            source = tid(dx, fy, fc)
            arrived(wo_recv.at[source], r_wo.at[source])

    def mix(j):
        total = jnp.zeros((part, LANE), F32)
        for dx, fy in order:
            slot_wait(ab, r_ab, j, tid(dx, fy, 1))
            if j == 0:
                out_wait(dx, fy, 0)
                out_wait(dx, fy, 1)
            k = tid(dx, fy, 0) // 2
            weights = jnp.concatenate([wo_recv[2 * k], wo_recv[2 * k + 1]], axis=1)
            heads = ab[j, pl.ds(2 * k, 2)].reshape(2 * HD, LANE)
            total = total + jnp.dot(weights, heads, preferred_element_type=F32)
        lanes = slice(j * LANE, (j + 1) * LANE)
        out_ref[:, lanes] = (xr[j].astype(F32) + modc[2] * total).astype(BF16)

    wo_recv[t] = wo_send[t]
    finish(0)
    finish(1)
    finish(2)
    relay_y(ab, r_ab, 0)
    relay_y(ab, r_ab, 1)
    relay_y(ab, r_ab, 2)
    relay_far(ab, r_ab, 0)
    relay_sides(ab, r_ab, 0)
    relay_far(ab, r_ab, 1)
    relay_sides(ab, r_ab, 1)
    relay_far(ab, r_ab, 2)
    relay_sides(ab, r_ab, 2)
    late(ab, r_ab, 0)
    mix(0)
    late(ab, r_ab, 1)
    mix(1)
    late(ab, r_ab, 2)
    mix(2)
    for copy in sends:
        copy.wait_send()


def local(frames_in, fresh, levels, reach, level_mod, w_qkv, q_gain, k_gain, w_out):
    queues = lax.axis_size("queue")
    tokens, part = fresh.shape
    model = w_qkv.shape[0]
    blocks = tokens // LANE
    vmem = pltpu.VMEM
    dma = pltpu.SemaphoreType.DMA
    any_spec = pl.BlockSpec(memory_space=pl.ANY)
    out = pl.pallas_call(
        lambda *refs: kernel(queues, *refs),
        out_shape=pltpu.VMEM((part, tokens), BF16),
        in_specs=[pl.BlockSpec(memory_space=pltpu.HBM)] * 2 + [any_spec] * 7,
        out_specs=pl.BlockSpec(memory_space=pltpu.VMEM),
        scratch_shapes=[
            vmem((blocks, part, LANE), BF16),
            vmem((blocks, part, LANE), BF16),
            vmem((8, LANE), F32),
            vmem((16, 8, LANE), F32),
            vmem((3, part, LANE), BF16),
            vmem((3, part, 1), F32),
            vmem((3, model, LANE), BF16),
            vmem((8, 3 * HD, 2 * part), BF16),
            vmem((blocks, 16, part, LANE), BF16),
            vmem((HD, tokens), BF16),
            vmem((7, blocks, 2, HD, HD), BF16),
            vmem((8, tokens), F32),
            vmem((8, tokens), F32),
            vmem((HD, tokens), F32),
            vmem((blocks, 16, HD, LANE), BF16),
            vmem((HD, model), BF16),
            vmem((16, part, HD), BF16),
            vmem((16, part, HD), BF16),
            vmem((16, LANE), F32),
            pltpu.SMEM((1,), jnp.int32),
            pltpu.SMEM((1,), jnp.int32),
            dma((16,)),
            dma((160,)),
            dma((blocks,)),
            dma((16,)),
            dma((blocks, 16)),
            dma((7, blocks)),
            dma((blocks, 16)),
            dma((16,)),
        ],
        compiler_params=pltpu.CompilerParams(
            collective_id=0, has_side_effects=True, vmem_limit_bytes=56 * 1024 * 1024
        ),
        name="block",
    )(
        levels, reach, frames_in[0].T, fresh.T, jnp.transpose(level_mod, (1, 2, 0)),
        jnp.transpose(w_qkv, (1, 0, 2)), q_gain.reshape(1, HD), k_gain.reshape(1, HD), w_out,
    )
    return out.T[None]


def solution(mesh):
    return jax.shard_map(
        local,
        mesh=mesh,
        in_specs=(
            P("queue", None, "tensor"),
            P(None, "tensor"),
            P("queue"),
            P("queue"),
            P(None, None, "tensor"),
            P(None, None, "tensor"),
            P("tensor"),
            P("tensor"),
            P("tensor", None),
        ),
        out_specs=P("queue", None, "tensor"),
        check_vma=False,
    )
```
